512 devices in a mesh: tm: 32 (over z, x_hi), space: 16 (over y, x_lo, core).
Axes of the slice: x: 4 (x_hi: 2, x_lo: 2; x = x_hi * 2 + x_lo), y: 4, z: 16, core: 2. Of those that a mesh axis runs over, the one named last changes fastest.
Arguments:
- multiplier: bfloat16 [32, 1280, 2560], P('tm', 'space'), may hold values from -6 to 6
- increment: bfloat16 [32, 1280, 2560], P('tm', 'space'), may hold values from -6 to 6
- wind_east: bfloat16 [32, 1280, 2560], P('tm', 'space'), may hold values from -0.3984375 to 0.3984375
- wind_north: bfloat16 [32, 1280, 2560], P('tm', 'space'), may hold values from -0.3984375 to 0.3984375
- variances: bfloat16 [32, 1280, 2560], P('tm', None, 'space'), may hold values from 0.3 to 36, as said below
Outputs:
- multiplier_out: bfloat16 [32, 1280, 2560], P('tm', 'space')
- increment_out: bfloat16 [32, 1280, 2560], P('tm', 'space')
The draws below stay inside these ranges and needn't reach their ends.
Inputs may be any that keep to these rules, and one draw needn't show every extreme that they name: `variances`: positive.
All inputs are finite; a program needn't handle non-finite values.
Results may differ from the reference program's by a relative error of at most 0.0055.
The reference program's roundings to bfloat16 on the way (of `longitude_table`, `latitude_table`, `coeffs`, `scaled` and `returned`) count: a program that leaves them out, or rounds other values in their place, can miss the bound.
Values may be sent and summed in bfloat16 or wider, within the bound.
A program may use at most 128 MiB of HBM per device.

```python
import math
import jax
import jax.numpy as jnp
from jax import lax

NLAT = 1280
NLON = 2560
STEPS = 4
SUBWIN = 32


def draw_variances(key, part):
    key = jax.random.fold_in(key, 7)
    lat_wave = jnp.arange(NLAT, dtype=jnp.float32)[:, None]
    col_index = jnp.arange(NLON, dtype=jnp.int32)[None, :]
    lon_wave = jnp.where(col_index <= NLON // 2, col_index, col_index - NLON // 2).astype(jnp.float32)
    rough = jnp.exp(jax.random.uniform(key, (SUBWIN, NLAT, NLON), jnp.float32, -1.2, 1.2))
    smooth = 1.0 + 4.0 * jnp.exp(-(lat_wave + lon_wave) / 64.0)
    return (rough * smooth).astype(jnp.bfloat16)


def block_scale(stream_key, extent, pieces, low, high):
    loudness, own = 1.0, jax.random.fold_in(stream_key, 6)
    for axis_at, parts in pieces:
        steps = jnp.exp(jax.random.uniform(jax.random.fold_in(own, axis_at), (parts,), jnp.float32, low / len(pieces), high / len(pieces)))
        loudness = loudness * jnp.repeat(steps, extent[axis_at] // parts).reshape([-1 if axis == axis_at else 1 for axis in range(len(extent))])
    return loudness


def noise(rng, dims, deviation, most, cuts=(), held_as=jnp.bfloat16):
    values = jax.random.normal(rng, dims, jnp.float32) * deviation
    if len(cuts) > 0:
        values = block_scale(rng, dims, cuts, -0.22, 0.18) * values
    return jnp.clip(values, min=-most, max=most).astype(held_as)


def setup_inputs(seed: int = 0) -> dict:
    streams_of = jax.random.split(jax.random.key(seed), 6)
    return {
        "multiplier": noise(streams_of[0], (SUBWIN, NLAT, NLON), 1.0, 6.0, ((0, 32), (1, 16))),
        "increment": noise(streams_of[1], (SUBWIN, NLAT, NLON), 1.0, 6.0, ((0, 32), (1, 16))),
        "wind_east": jnp.clip(jax.random.uniform(streams_of[2], (SUBWIN, NLAT, NLON), jnp.float32, -0.3984375, 0.3984375) * block_scale(streams_of[2], (SUBWIN, NLAT, NLON), ((0, 32), (1, 16)), -0.4, 0.0), -0.3984375, 0.3984375).astype(jnp.bfloat16),
        "wind_north": jnp.clip(jax.random.uniform(streams_of[3], (SUBWIN, NLAT, NLON), jnp.float32, -0.3984375, 0.3984375) * block_scale(streams_of[3], (SUBWIN, NLAT, NLON), ((0, 32), (1, 16)), -0.4, 0.0), -0.3984375, 0.3984375).astype(jnp.bfloat16),
        "variances": draw_variances(jax.random.fold_in(streams_of[5], 71), 0),
    }


DIFFUSION = 0.2

def stencil_weights(wind_east, wind_north):
    eastern = wind_east.astype(jnp.float32) * 0.5
    northern = wind_north.astype(jnp.float32) * 0.5
    return (DIFFUSION - eastern, DIFFUSION + eastern, DIFFUSION - northern, DIFFUSION + northern)

def longitude_table(block_start, block_width, length):
    row_index = lax.broadcasted_iota(jnp.int32, (length, block_width), 0)
    col_index = lax.broadcasted_iota(jnp.int32, (length, block_width), 1) + block_start
    half_len = length // 2
    wavenumber = jnp.where(col_index <= half_len, col_index, col_index - half_len)
    phase = wavenumber * row_index % length
    phase_angle = phase.astype(jnp.float32) * (2.0 * math.pi / length)
    norm_scale = jnp.where((col_index == 0) | (col_index == half_len), math.sqrt(1.0 / length), math.sqrt(2.0 / length))
    entries = jnp.where(col_index <= half_len, jnp.cos(phase_angle), jnp.sin(phase_angle)) * norm_scale
    return entries.astype(jnp.bfloat16)

def latitude_table(length):
    mode_index = lax.broadcasted_iota(jnp.int32, (length, length), 0)
    row_index = lax.broadcasted_iota(jnp.int32, (length, length), 1)
    phase = mode_index * (2 * row_index + 1) % (4 * length)
    phase_angle = phase.astype(jnp.float32) * (math.pi / (2.0 * length))
    norm_scale = jnp.where(mode_index == 0, math.sqrt(1.0 / length), math.sqrt(2.0 / length))
    return (jnp.cos(phase_angle) * norm_scale).astype(jnp.bfloat16)

def forward_model(state, weights):
    eastward, westward, northward, southward = weights
    centre = 1.0 - 4.0 * DIFFUSION
    for step_index in range(STEPS):
        padded = jnp.pad(state, ((1, 1), (0, 0)))
        state = centre * state + eastward * jnp.roll(state, -1, 1) + westward * jnp.roll(state, 1, 1) + northward * padded[2:] + southward * padded[:-2]
    return state

def adjoint_model(state, weights):
    eastward, westward, northward, southward = weights
    centre = 1.0 - 4.0 * DIFFUSION
    for step_index in range(STEPS):
        padded_north = jnp.pad(northward * state, ((1, 1), (0, 0)))
        padded_south = jnp.pad(southward * state, ((1, 1), (0, 0)))
        state = centre * state + jnp.roll(eastward * state, 1, 1) + jnp.roll(westward * state, -1, 1) + padded_north[:-2] + padded_south[2:]
    return state

def reference(multiplier, increment, wind_east, wind_north, variances):
    lon_full = longitude_table(0, NLON, NLON)
    lat_full = latitude_table(NLAT)

    def one_window(index):
        previous_index = jnp.maximum(index - 1, 0).astype(jnp.int32)
        next_index = jnp.minimum(index + 1, SUBWIN - 1).astype(jnp.int32)
        weights = stencil_weights(wind_east[index], wind_north[index])
        next_weights = stencil_weights(wind_east[next_index], wind_north[next_index])
        forward = forward_model(increment[previous_index].astype(jnp.float32), weights)
        forward = jnp.where(index > 0, forward, jnp.zeros_like(forward))
        adjoint = adjoint_model(multiplier[next_index].astype(jnp.float32), next_weights)
        adjoint = jnp.where(index < SUBWIN - 1, adjoint, jnp.zeros_like(adjoint))
        coeffs = jnp.dot(multiplier[index], lon_full, preferred_element_type=jnp.float32).astype(jnp.bfloat16)
        scaled = (jnp.dot(lat_full, coeffs, preferred_element_type=jnp.float32) * variances[index].astype(jnp.float32)).astype(jnp.bfloat16)
        returned = jnp.dot(lat_full.T, scaled, preferred_element_type=jnp.float32).astype(jnp.bfloat16)
        covariance_term = jnp.dot(returned, lon_full.T, preferred_element_type=jnp.float32)
        first_row = (covariance_term + increment[index].astype(jnp.float32) - forward).astype(jnp.bfloat16)
        last_row = (multiplier[index].astype(jnp.float32) - adjoint).astype(jnp.bfloat16)
        return (first_row, last_row)
    multiplier_out, increment_out = lax.map(one_window, jnp.arange(SUBWIN, dtype=jnp.int32))
    return (multiplier_out, increment_out)
```

```python
import functools
import math

import jax
import jax.numpy as jnp
import ml_dtypes
import numpy as np
from jax import lax
from jax.experimental import pallas as pl
from jax.experimental.pallas import tpu as pltpu
from jax.sharding import PartitionSpec as P

STEPS = 4
DIFFUSION = 0.2
MESH = pl.DeviceIdType.MESH

ROWS = 80
NLON = 2560
NLAT = 1280
SPACE = 16
OWN = NLON // SPACE
MAIN = 128
TAIL = OWN - MAIN
MSG = 112
TOP = 16
PADDED = ROWS + 32
CHUNK = 256
CHUNKS = NLON // CHUNK
F32 = jnp.float32
BF16 = jnp.bfloat16


def longitude_table():
    row = np.arange(NLON)[:, None]
    col = np.arange(NLON)[None, :]
    half = NLON // 2
    wave = np.where(col <= half, col, col - half)
    angle = (wave * row % NLON) * (2.0 * math.pi / NLON)
    scale = np.where((col == 0) | (col == half), math.sqrt(1.0 / NLON), math.sqrt(2.0 / NLON))
    return (np.where(col <= half, np.cos(angle), np.sin(angle)) * scale).astype(ml_dtypes.bfloat16)


def latitude_table():
    mode = np.arange(NLAT)[:, None]
    row = np.arange(NLAT)[None, :]
    angle = (mode * (2 * row + 1) % (4 * NLAT)) * (math.pi / (2.0 * NLAT))
    scale = np.where(mode == 0, math.sqrt(1.0 / NLAT), math.sqrt(2.0 / NLAT))
    return (np.cos(angle) * scale).astype(ml_dtypes.bfloat16)


def column_order():
    first = [OWN * d + np.arange(MAIN) for d in range(SPACE)]
    last = [OWN * d + MAIN + np.arange(TAIL) for d in range(SPACE)]
    return np.concatenate(first + last)


@functools.lru_cache(maxsize=1)
def tables():
    lon = longitude_table()
    lat = latitude_table()
    order = column_order()
    forward = lon[:, order].reshape(NLON, CHUNKS, CHUNK).transpose(1, 0, 2)
    inverse = lon.T[order, :].reshape(NLON, CHUNKS, CHUNK).transpose(1, 0, 2)
    return (
        np.ascontiguousarray(forward),
        np.ascontiguousarray(inverse),
        np.ascontiguousarray(lat.reshape(4, 320, NLAT)),
        np.ascontiguousarray(lat.T.reshape(4, 320, NLAT)),
    )


def lane_group(shape):
    return lax.broadcasted_iota(jnp.int32, shape, 1) // TAIL


def turned(x, shift):
    shift = shift % x.shape[1]
    return x if shift == 0 else pltpu.roll(x, shift, 1)


def packed_tail(groups, from_group):
    place = lane_group((16, 128))
    head = jnp.zeros((16, 128), F32)
    for g in range(4):
        head = jnp.where(place == g, turned(groups[g], TAIL * (g - from_group)), head)
    last = turned(groups[4], TAIL * (0 - from_group))
    return jnp.concatenate([head, last], axis=0).astype(BF16)


def kernel(
    windows,
    mult_h, inc_h, east_h, north_h, var_h, lonf_h, loni_h, lat_h, latt_h,
    out1_h, out2_h,
    mult_v, inc_v, east_v, north_v, var_v, lonf_v, loni_v, lat_v, latt_v,
    inc_r, inc_edge_s, inc_edge_r, edge_s, edge_r, adj_s, adj_r,
    state, half_e, half_n,
    send1, recv1, send2, recv2,
    cols, scaled, grid, varf, out1_v, out2_v,
    load_sem, lonf_sem, loni_sem, out_sem,
    inc_ss, inc_rs, iedge_ss, iedge_rs, edge_ss, edge_rs, adj_ss, adj_rs,
    a1_ss, a1_rs, a2_ss, a2_rs,
):
    tm = lax.axis_index("tm")
    me = lax.axis_index("space")
    after = lax.rem(tm + 1, windows)
    before = lax.rem(tm + windows - 1, windows)
    up = lax.rem(me + SPACE - 1, SPACE)
    down = lax.rem(me + 1, SPACE)
    core = lax.rem(me, 2)
    chip = me // 2
    sibling = me + 1 - 2 * core
    band = me // 4
    seat = lax.rem(me, 4)

    barrier = pltpu.get_barrier_semaphore()
    for o in range(1, SPACE):
        pl.semaphore_signal(
            barrier, inc=1, device_id=(tm, lax.rem(me + o, SPACE)), device_id_type=MESH
        )
    for window in (after, before):
        for space in (me, up, down):
            pl.semaphore_signal(barrier, inc=1, device_id=(window, space), device_id_type=MESH)

    def load(src, dst, sem):
        copy = pltpu.make_async_copy(src, dst, sem)
        copy.start()
        return copy

    loads = {
        name: load(src, dst, load_sem.at[n])
        for n, (name, src, dst) in enumerate(
            (
                ("mult", mult_h, mult_v),
                ("inc", inc_h, inc_v),
                ("east", east_h, east_v),
                ("north", north_h, north_v),
                ("var", var_h, var_v),
            )
        )
    }
    lonf_loads = [load(lonf_h.at[8 + t], lonf_v.at[8 + t], lonf_sem.at[8 + t]) for t in range(2)]
    for j in range(8):
        which = lax.rem(chip + 1 + j, 8)
        lonf_loads.append(load(lonf_h.at[which], lonf_v.at[j], lonf_sem.at[j]))
    lat_load = load(lat_h, lat_v, load_sem.at[5])
    latt_load = load(latt_h, latt_v, load_sem.at[6])
    loni_loads = [load(loni_h.at[n], loni_v.at[n], loni_sem.at[n]) for n in range(CHUNKS)]

    pl.semaphore_wait(barrier, 21)

    inc_copy = pltpu.make_async_remote_copy(
        src_ref=inc_h, dst_ref=inc_r, send_sem=inc_ss, recv_sem=inc_rs,
        device_id=(after, me), device_id_type=MESH,
    )
    inc_copy.start()

    def edges(ref):
        first = ref[0:16, :].astype(F32)[0:STEPS]
        last = ref[ROWS - 16 : ROWS, :].astype(F32)[16 - STEPS : 16]
        return first, last

    def folded(rows):
        return jnp.concatenate([rows[:, 640 * q : 640 * (q + 1)] for q in range(4)], axis=0)

    for name in ("mult", "inc", "east", "north"):
        loads[name].wait()
    parts = [edges(ref) for ref in (mult_v, east_v, north_v)]
    blank = jnp.zeros((16 - 3 * STEPS, NLON), F32)
    for side in range(2):
        edge_s[side] = jnp.concatenate([part[side] for part in parts] + [blank], axis=0).astype(BF16)
    own_edges = edges(inc_v)
    for side in range(2):
        inc_edge_s[side] = folded(own_edges[side]).astype(BF16)
    edge_copies = []
    for side, space in ((0, up), (1, down)):
        edge_copies.append(
            pltpu.make_async_remote_copy(
                src_ref=edge_s.at[side], dst_ref=edge_r.at[1 - side],
                send_sem=edge_ss.at[side], recv_sem=edge_rs.at[1 - side],
                device_id=(tm, space), device_id_type=MESH,
            )
        )
        edge_copies.append(
            pltpu.make_async_remote_copy(
                src_ref=inc_edge_s.at[side], dst_ref=inc_edge_r.at[1 - side],
                send_sem=iedge_ss.at[side], recv_sem=iedge_rs.at[1 - side],
                device_id=(after, space), device_id_type=MESH,
            )
        )
    for copy in edge_copies:
        copy.start()

    for t in range(2):
        lonf_loads[t].wait()
        product = jnp.dot(mult_v[...], lonf_v[8 + t], preferred_element_type=F32)
        for q in range(2):
            tile = product[:, 128 * q : 128 * (q + 1)]
            groups = [tile[16 * g : 16 * (g + 1)] for g in range(5)]
            for r in range(4):
                recv_slot = 4 * (2 * t + q) + r
                slot = 2 * lax.rem(recv_slot // 2 + 15 - chip, 8) + recv_slot % 2
                send1[slot, ROWS:MSG, :] = packed_tail(groups, r)

    def a1_copy(slot, owner):
        return pltpu.make_async_remote_copy(
            src_ref=send1.at[slot], dst_ref=recv1.at[me],
            send_sem=a1_ss.at[slot], recv_sem=a1_rs.at[me],
            device_id=(tm, owner), device_id_type=MESH,
        )

    def lon_step(j, _):
        which = lax.rem(chip + 1 + j, 8)
        pltpu.make_async_copy(lonf_h.at[which], lonf_v.at[j], lonf_sem.at[j]).wait()
        product = jnp.dot(mult_v[...], lonf_v[j], preferred_element_type=F32).astype(BF16)
        for c in range(2):
            send1[2 * j + c, 0:ROWS, :] = product[:, 128 * c : 128 * (c + 1)]

        @pl.when(j < 7)
        def _():
            for c in range(2):
                a1_copy(2 * j + c, 2 * which + c).start()

        return 0

    lax.fori_loop(0, 8, lon_step, 0)
    a1_copy(14 + 1 - core, sibling).start()
    recv1[me] = send1[14 + core]

    for ref, src in ((half_e, east_v), (half_n, north_v)):
        ref[TOP : TOP + ROWS, :] = src[...].astype(F32) * 0.5
    state[0, TOP : TOP + ROWS, :] = mult_v[...].astype(F32)
    for side in range(2):
        edge_copies[2 * side].wait_recv()
    gap = jnp.zeros((8 - STEPS, NLON), F32)

    def outside(side, rows):
        parts = [gap, rows] if side == 0 else [rows, gap]
        return jnp.concatenate(parts, axis=0)

    halo_at = (TOP - 8, TOP + ROWS)
    inside = (me > 0, me < SPACE - 1)
    for side in range(2):
        rows = edge_r[side].astype(F32)
        at = pl.ds(halo_at[side], 8)
        state[0, at, :] = jnp.where(inside[side], outside(side, rows[0:STEPS]), 0.0)
        half_e[at, :] = outside(side, rows[STEPS : 2 * STEPS]) * 0.5
        half_n[at, :] = outside(side, rows[2 * STEPS : 3 * STEPS]) * 0.5

    sublane = lax.broadcasted_iota(jnp.int32, (8, NLON), 0)

    def near(ref, r):
        return ref[pl.ds(r - 8, 8), :], ref[pl.ds(r, 8), :], ref[pl.ds(r + 8, 8), :]

    def row_above(before, x):
        return pltpu.roll(jnp.where(sublane == 7, before, x), 1, 0)

    def row_below(x, behind):
        return pltpu.roll(jnp.where(sublane == 0, behind, x), 7, 0)

    def forward_strip(src, r):
        before, x, behind = near(src, r)
        above = row_above(before, x)
        below = row_below(x, behind)
        east = pltpu.roll(x, NLON - 1, 1)
        west = pltpu.roll(x, 1, 1)
        return (
            DIFFUSION * ((x + (east + west)) + (above + below))
            + half_e[pl.ds(r, 8), :] * (west - east)
            + half_n[pl.ds(r, 8), :] * (above - below)
        )

    def adjoint_strip(src, r):
        before, y, behind = near(src, r)
        n_before, n, n_behind = near(half_n, r)
        fifth = DIFFUSION * y
        zonal = half_e[pl.ds(r, 8), :] * y
        merid = n * y
        north = row_above((DIFFUSION - n_before) * before, fifth - merid)
        south = row_below(fifth + merid, (DIFFUSION + n_behind) * behind)
        return (
            (fifth + (north + south))
            + (pltpu.roll(fifth - zonal, 1, 1) + pltpu.roll(fifth + zonal, NLON - 1, 1))
        )

    def steps(strip):
        for step in range(STEPS):
            src, dst = state.at[step % 2], state.at[(step + 1) % 2]
            whole = step < STEPS - 1

            def one(i, _):
                r = pl.multiple_of(8 * i + (TOP - 8 if whole else TOP), 8)
                dst[pl.ds(r, 8), :] = strip(src, r)
                return 0

            lax.fori_loop(0, ROWS // 8 + (2 if whole else 0), one, 0)
            if whole:
                for side in range(2):
                    at = pl.ds(halo_at[side], 8)
                    dst[at, :] = jnp.where(inside[side], dst[at, :], 0.0)

    for at in (TOP - 16, TOP + ROWS + 8):
        for ref in (state.at[0], state.at[1], half_n):
            ref[pl.ds(at, 8), :] = jnp.zeros((8, NLON), F32)
    steps(adjoint_strip)
    adj_s[...] = state[0, TOP : TOP + ROWS, :].astype(BF16)
    adj_copy = pltpu.make_async_remote_copy(
        src_ref=adj_s, dst_ref=adj_r, send_sem=adj_ss, recv_sem=adj_rs,
        device_id=(before, me), device_id_type=MESH,
    )
    adj_copy.start()

    loads["var"].wait()
    varf[:, 0:OWN] = var_v[...].astype(F32).T
    varf[:, OWN:CHUNK] = jnp.zeros((NLAT, CHUNK - OWN), F32)
    lat_load.wait()
    latt_load.wait()

    def gather(o, _):
        source = lax.rem(me + o, SPACE)

        @pl.when(o > 0)
        def _():
            pltpu.make_async_remote_copy(
                src_ref=send1.at[0], dst_ref=recv1.at[source],
                send_sem=a1_ss.at[0], recv_sem=a1_rs.at[source],
                device_id=(tm, source), device_id_type=MESH,
            ).wait_recv()

        at = pl.multiple_of(source * ROWS, 16)
        cols[pl.ds(at, ROWS), 0:MAIN] = recv1[source, 0:ROWS, :]
        tail = recv1[source, ROWS:MSG, :].astype(F32)
        for g in range(5):
            rows = turned(tail[0:16], -TAIL * g) if g < 4 else tail[16:32]
            cols[pl.ds(pl.multiple_of(at + 16 * g, 16), 16), MAIN:CHUNK] = rows.astype(BF16)
        return 0

    lax.fori_loop(0, SPACE, gather, 0)

    def lat_step(m, _):
        at = pl.ds(pl.multiple_of(m * 320, 320), 320)
        product = jnp.dot(lat_v[m], cols[...], preferred_element_type=F32)
        scaled[at, :] = (product * varf[at, :]).astype(BF16)
        return 0

    lax.fori_loop(0, 4, lat_step, 0)

    def a2_copy(slot, owner):
        return pltpu.make_async_remote_copy(
            src_ref=send2.at[slot], dst_ref=recv2.at[me],
            send_sem=a2_ss.at[slot], recv_sem=a2_rs.at[me],
            device_id=(tm, owner), device_id_type=MESH,
        )

    def back_step(j, _):
        q = lax.rem(band + 1 + j, 4)
        product = jnp.dot(latt_v[q], scaled[...], preferred_element_type=F32)
        for r in range(4):
            block = product[ROWS * r : ROWS * (r + 1)]
            tile = block[:, MAIN:CHUNK]
            send2[4 * j + r, 0:ROWS, :] = block[:, 0:MAIN].astype(BF16)
            send2[4 * j + r, ROWS:MSG, :] = packed_tail(
                [tile[16 * g : 16 * (g + 1)] for g in range(5)], 0
            )

        @pl.when(j < 3)
        def _():
            for r in range(4):
                a2_copy(4 * j + r, 4 * q + r).start()

        return 0

    lax.fori_loop(0, 4, back_step, 0)
    for o in range(1, 4):
        other = lax.rem(seat + o, 4)
        a2_copy(12 + other, 4 * band + other).start()
    recv2[me] = send2[12 + seat]

    inc_copy.wait_recv()
    for side in range(2):
        edge_copies[2 * side + 1].wait_recv()
    state[0, TOP : TOP + ROWS, :] = inc_r[...].astype(F32)
    for side in range(2):
        rows = inc_edge_r[side].astype(F32)
        rows = jnp.concatenate([rows[STEPS * q : STEPS * (q + 1)] for q in range(4)], axis=1)
        state[0, pl.ds(halo_at[side], 8), :] = jnp.where(inside[side], outside(side, rows), 0.0)
    steps(forward_strip)

    adj_copy.wait_recv()
    kept = jnp.where(tm < windows - 1, 1.0, 0.0)
    out2_v[...] = (mult_v[...].astype(F32) - kept * adj_r[...].astype(F32)).astype(BF16)
    out2_copy = load(out2_v, out2_h, out_sem.at[0])

    for source in range(SPACE):

        @pl.when(source != me)
        def _():
            pltpu.make_async_remote_copy(
                src_ref=send2.at[0], dst_ref=recv2.at[source],
                send_sem=a2_ss.at[0], recv_sem=a2_rs.at[source],
                device_id=(tm, me), device_id_type=MESH,
            ).wait_recv()

    place = lane_group((16, 128))
    for q in range(4):
        tails = []
        for r in range(4):
            source = 4 * q + r
            grid[:, MAIN * source : MAIN * (source + 1)] = recv2[source, 0:ROWS, :]
            tails.append(recv2[source, ROWS:MSG, :].astype(F32))
        for g in range(5):
            rows = jnp.zeros((16, 128), F32)
            for r in range(4):
                part = tails[r][0:16] if g < 4 else tails[r][16:32]
                rows = jnp.where(place == r, turned(part, TAIL * (r - g % 4)), rows)
            at = SPACE * MAIN + 128 * q
            grid[16 * g : 16 * (g + 1), at : at + 128] = rows.astype(BF16)

    taken = jnp.where(tm > 0, 1.0, 0.0)

    def out_step(n, _):
        pltpu.make_async_copy(loni_h.at[n], loni_v.at[n], loni_sem.at[n]).wait()
        at = pl.ds(pl.multiple_of(n * CHUNK, CHUNK), CHUNK)
        term = jnp.dot(grid[...], loni_v[n], preferred_element_type=F32)
        ahead = state[0, TOP : TOP + ROWS, at]
        out1_v[:, at] = (term + inc_v[:, at].astype(F32) - taken * ahead).astype(BF16)
        return 0

    lax.fori_loop(0, CHUNKS, out_step, 0)
    out1_copy = load(out1_v, out1_h, out_sem.at[1])

    inc_copy.wait_send()
    for copy in edge_copies:
        copy.wait_send()
    adj_copy.wait_send()

    def sent(slot, _):
        for src, dst, ss, rs in ((send1, recv1, a1_ss, a1_rs), (send2, recv2, a2_ss, a2_rs)):
            own = (14 + core) if ss is a1_ss else (12 + seat)

            @pl.when(slot != own)
            def _():
                pltpu.make_async_remote_copy(
                    src_ref=src.at[slot], dst_ref=dst.at[me],
                    send_sem=ss.at[slot], recv_sem=rs.at[me],
                    device_id=(tm, sibling), device_id_type=MESH,
                ).wait_send()

        return 0

    lax.fori_loop(0, SPACE, sent, 0)
    out2_copy.wait()
    out1_copy.wait()


def shards(windows, multiplier, increment, wind_east, wind_north, variances):
    lonf, loni, lat, latt = (jnp.asarray(table) for table in tables())
    block = (ROWS, NLON)
    wide = (PADDED, NLON)
    dma = pltpu.SemaphoreType.DMA
    vmem = pltpu.VMEM
    first, last = pl.pallas_call(
        functools.partial(kernel, windows),
        out_shape=(jax.ShapeDtypeStruct(block, BF16), jax.ShapeDtypeStruct(block, BF16)),
        in_specs=[pl.BlockSpec(memory_space=pl.ANY)] * 9,
        out_specs=(pl.BlockSpec(memory_space=pl.ANY),) * 2,
        scratch_shapes=[
            vmem(block, BF16), vmem(block, BF16), vmem(block, BF16), vmem(block, BF16),
            vmem((OWN, NLAT), BF16),
            vmem((CHUNKS, NLON, CHUNK), BF16), vmem((CHUNKS, NLON, CHUNK), BF16),
            vmem((4, 320, NLAT), BF16), vmem((4, 320, NLAT), BF16),
            vmem(block, BF16), vmem((2, 16, 640), BF16), vmem((2, 16, 640), BF16),
            vmem((2, 16, NLON), BF16), vmem((2, 16, NLON), BF16),
            vmem(block, BF16), vmem(block, BF16),
            vmem((2, *wide), F32), vmem(wide, F32), vmem(wide, F32),
            vmem((SPACE, MSG, 128), BF16), vmem((SPACE, MSG, 128), BF16),
            vmem((SPACE, MSG, 128), BF16), vmem((SPACE, MSG, 128), BF16),
            vmem((NLAT, CHUNK), BF16), vmem((NLAT, CHUNK), BF16), vmem(block, BF16),
            vmem((NLAT, CHUNK), F32), vmem(block, BF16), vmem(block, BF16),
            dma((7,)), dma((CHUNKS,)), dma((CHUNKS,)), dma((2,)),
            dma, dma, dma((2,)), dma((2,)), dma((2,)), dma((2,)), dma, dma,
            dma((SPACE,)), dma((SPACE,)), dma((SPACE,)), dma((SPACE,)),
        ],
        compiler_params=pltpu.CompilerParams(
            collective_id=0, has_side_effects=True, vmem_limit_bytes=60 * 2**20
        ),
        cost_estimate=pl.CostEstimate(
            flops=3_145_728_000, bytes_accessed=36_000_000, transcendentals=0
        ),
    )(
        multiplier[0], increment[0], wind_east[0], wind_north[0],
        jnp.swapaxes(variances[0], 0, 1), lonf, loni, lat, latt,
    )
    return first[None], last[None]


def solution(mesh):
    placed = P("tm", "space", None)
    return jax.shard_map(
        functools.partial(shards, mesh.shape["tm"]),
        mesh=mesh,
        in_specs=(placed, placed, placed, placed, P("tm", None, "space")),
        out_specs=(placed, placed),
        check_vma=False,
    )
```

```python
import functools
import math

import jax
import jax.numpy as jnp
import ml_dtypes
import numpy as np
from jax import lax
from jax.experimental import pallas as pl
from jax.experimental.pallas import tpu as pltpu
from jax.sharding import PartitionSpec as P

STEPS = 4
DIFFUSION = 0.2
MESH = pl.DeviceIdType.MESH

ROWS = 80
NLON = 2560
NLAT = 1280
SPACE = 16
OWN = NLON // SPACE
MAIN = 128
TAIL = OWN - MAIN
MSG = 112
TOP = 16
PADDED = ROWS + 32
CHUNK = 256
CHUNKS = NLON // CHUNK
INC_CUT = 16
ADJ_CUT = 64
F32 = jnp.float32
BF16 = jnp.bfloat16


def longitude_table():
    row = np.arange(NLON)[:, None]
    col = np.arange(NLON)[None, :]
    half = NLON // 2
    wave = np.where(col <= half, col, col - half)
    angle = (wave * row % NLON) * (2.0 * math.pi / NLON)
    scale = np.where((col == 0) | (col == half), math.sqrt(1.0 / NLON), math.sqrt(2.0 / NLON))
    return (np.where(col <= half, np.cos(angle), np.sin(angle)) * scale).astype(ml_dtypes.bfloat16)


def latitude_table():
    mode = np.arange(NLAT)[:, None]
    row = np.arange(NLAT)[None, :]
    angle = (mode * (2 * row + 1) % (4 * NLAT)) * (math.pi / (2.0 * NLAT))
    scale = np.where(mode == 0, math.sqrt(1.0 / NLAT), math.sqrt(2.0 / NLAT))
    return (np.cos(angle) * scale).astype(ml_dtypes.bfloat16)


def column_order():
    first = [OWN * d + np.arange(MAIN) for d in range(SPACE)]
    last = [OWN * d + MAIN + np.arange(TAIL) for d in range(SPACE)]
    return np.concatenate(first + last)


@functools.lru_cache(maxsize=1)
def tables():
    lon = longitude_table()
    lat = latitude_table()
    order = column_order()
    forward = lon[:, order].reshape(NLON, CHUNKS, CHUNK).transpose(1, 0, 2)
    inverse = lon.T[order, :].reshape(NLON, CHUNKS, CHUNK).transpose(1, 0, 2)
    return (
        np.ascontiguousarray(forward),
        np.ascontiguousarray(inverse),
        np.ascontiguousarray(lat.reshape(4, 320, NLAT)),
        np.ascontiguousarray(lat.T.reshape(4, 320, NLAT)),
    )


def lane_group(shape):
    return lax.broadcasted_iota(jnp.int32, shape, 1) // TAIL


def turned(x, shift):
    shift = shift % x.shape[1]
    return x if shift == 0 else pltpu.roll(x, shift, 1)


def packed_tail(groups, from_group):
    place = lane_group((16, 128))
    head = jnp.zeros((16, 128), F32)
    for g in range(4):
        head = jnp.where(place == g, turned(groups[g], TAIL * (g - from_group)), head)
    last = turned(groups[4], TAIL * (0 - from_group))
    return jnp.concatenate([head, last], axis=0).astype(BF16)


def kernel(
    windows,
    mult_h, inc_h, east_h, north_h, var_h, lonf_h, loni_h, lat_h, latt_h,
    out1_h, out2_h,
    mult_v, inc_v, east_v, north_v, var_v, lonf_v, loni_v, lat_v, latt_v,
    inc_r, inc_edge_s, inc_edge_r, edge_s, edge_r, adj_s, adj_r,
    state, state_b, half_e, half_n,
    send1, recv1, send2, recv2,
    cols, scaled, grid, varf, out1_v,
    load_sem, lonf_sem, loni_sem, out1_sem,
    inc_sem, iedge_ss, iedge_rs, edge_ss, edge_rs, adj_sem,
    a1_ss, a1_rs, a2_ss, a2_rs,
):
    tm = lax.axis_index("tm")
    me = lax.axis_index("space")
    after = lax.rem(tm + 1, windows)
    before = lax.rem(tm + windows - 1, windows)
    up = lax.rem(me + SPACE - 1, SPACE)
    down = lax.rem(me + 1, SPACE)
    core = lax.rem(me, 2)
    chip = me // 2
    sibling = me + 1 - 2 * core
    band = me // 4
    seat = lax.rem(me, 4)

    barrier = pltpu.get_barrier_semaphore()
    for o in range(1, SPACE):
        pl.semaphore_signal(
            barrier, inc=1, device_id=(tm, lax.rem(me + o, SPACE)), device_id_type=MESH
        )
    for window in (after, before):
        for space in (me, up, down):
            pl.semaphore_signal(barrier, inc=1, device_id=(window, space), device_id_type=MESH)

    def load(src, dst, sem):
        copy = pltpu.make_async_copy(src, dst, sem)
        copy.start()
        return copy

    loads = {
        name: load(src, dst, load_sem.at[n])
        for n, (name, src, dst) in enumerate(
            (
                ("mult", mult_h, mult_v),
                ("inc", inc_h, inc_v),
                ("east", east_h, east_v),
                ("north", north_h, north_v),
            )
        )
    }
    lonf_loads = [load(lonf_h.at[8 + t], lonf_v.at[8 + t], lonf_sem.at[8 + t]) for t in range(2)]
    for j in range(8):
        which = lax.rem(chip + 1 + j, 8)
        lonf_loads.append(load(lonf_h.at[which], lonf_v.at[j], lonf_sem.at[j]))

    pl.semaphore_wait(barrier, 21)

    def exchange(src, dst, sem, to, cut):
        return [
            pltpu.make_async_remote_copy(
                src_ref=src.at[rows], dst_ref=dst.at[rows],
                send_sem=sem.at[2 * n], recv_sem=sem.at[2 * n + 1],
                device_id=(to, me), device_id_type=MESH,
            )
            for n, rows in enumerate((pl.ds(0, cut), pl.ds(cut, ROWS - cut)))
        ]

    inc_copies = exchange(inc_h, inc_r, inc_sem, after, INC_CUT)
    adj_copies = exchange(adj_s, adj_r, adj_sem, before, ADJ_CUT)
    has_next, has_previous = tm < windows - 1, tm > 0

    def edges(ref):
        first = ref[0:16, :].astype(F32)[0:STEPS]
        last = ref[ROWS - 16 : ROWS, :].astype(F32)[16 - STEPS : 16]
        return first, last

    def folded(rows):
        return jnp.concatenate([rows[:, 640 * q : 640 * (q + 1)] for q in range(4)], axis=0)

    for name in ("mult", "inc", "east", "north"):
        loads[name].wait()
    parts = [edges(ref) for ref in (mult_v, east_v, north_v)]
    blank = jnp.zeros((16 - 3 * STEPS, NLON), F32)
    for side in range(2):
        edge_s[side] = jnp.concatenate([part[side] for part in parts] + [blank], axis=0).astype(BF16)
    own_edges = edges(inc_v)
    for side in range(2):
        inc_edge_s[side] = folded(own_edges[side]).astype(BF16)
    edge_copies = []
    for side, space in ((0, up), (1, down)):
        edge_copies.append(
            pltpu.make_async_remote_copy(
                src_ref=edge_s.at[side], dst_ref=edge_r.at[1 - side],
                send_sem=edge_ss.at[side], recv_sem=edge_rs.at[1 - side],
                device_id=(tm, space), device_id_type=MESH,
            )
        )
        edge_copies.append(
            pltpu.make_async_remote_copy(
                src_ref=inc_edge_s.at[side], dst_ref=inc_edge_r.at[1 - side],
                send_sem=iedge_ss.at[side], recv_sem=iedge_rs.at[1 - side],
                device_id=(after, space), device_id_type=MESH,
            )
        )
    for copy in (edge_copies[0], edge_copies[2]):
        copy.start()

    @pl.when(has_next)
    def _():
        for copy in (edge_copies[1], edge_copies[3]):
            copy.start()


    for t in range(2):
        lonf_loads[t].wait()
        product = jnp.dot(mult_v[...], lonf_v[8 + t], preferred_element_type=F32)
        for q in range(2):
            tile = product[:, 128 * q : 128 * (q + 1)]
            groups = [tile[16 * g : 16 * (g + 1)] for g in range(5)]
            for r in range(4):
                recv_slot = 4 * (2 * t + q) + r
                slot = 2 * lax.rem(recv_slot // 2 + 15 - chip, 8) + recv_slot % 2
                send1[slot, ROWS:MSG, :] = packed_tail(groups, r)

    def a1_copy(slot, owner):
        return pltpu.make_async_remote_copy(
            src_ref=send1.at[slot], dst_ref=recv1.at[me],
            send_sem=a1_ss.at[slot], recv_sem=a1_rs.at[me],
            device_id=(tm, owner), device_id_type=MESH,
        )

    def lon_step(j, _):
        which = lax.rem(chip + 1 + j, 8)
        pltpu.make_async_copy(lonf_h.at[which], lonf_v.at[j], lonf_sem.at[j]).wait()
        product = jnp.dot(mult_v[...], lonf_v[j], preferred_element_type=F32).astype(BF16)
        for c in range(2):
            send1[2 * j + c, 0:ROWS, :] = product[:, 128 * c : 128 * (c + 1)]

        @pl.when(j < 7)
        def _():
            for c in range(2):
                a1_copy(2 * j + c, 2 * which + c).start()

        return 0

    lax.fori_loop(0, 8, lon_step, 0)
    loads["var"] = load(var_h, var_v, load_sem.at[4])
    lat_load = load(lat_h, lat_v, load_sem.at[5])
    latt_load = load(latt_h, latt_v, load_sem.at[6])
    for n in range(CHUNKS):
        load(loni_h.at[n], loni_v.at[n], loni_sem.at[n])
    a1_copy(14 + 1 - core, sibling).start()
    recv1[me] = send1[14 + core]

    @pl.when(has_next)
    def _():
        for copy in inc_copies:
            copy.start()


    for ref, src in ((half_e, east_v), (half_n, north_v)):
        ref[TOP : TOP + ROWS, :] = src[...].astype(F32) * 0.5
    state[TOP : TOP + ROWS, :] = mult_v[...].astype(F32)
    for side in range(2):
        edge_copies[2 * side].wait_recv()
    gap = jnp.zeros((8 - STEPS, NLON), F32)

    def outside(side, rows):
        parts = [gap, rows] if side == 0 else [rows, gap]
        return jnp.concatenate(parts, axis=0)

    halo_at = (TOP - 8, TOP + ROWS)
    inside = (me > 0, me < SPACE - 1)
    for side in range(2):
        rows = edge_r[side].astype(F32)
        at = pl.ds(halo_at[side], 8)
        state[at, :] = jnp.where(inside[side], outside(side, rows[0:STEPS]), 0.0)
        half_e[at, :] = outside(side, rows[STEPS : 2 * STEPS]) * 0.5
        half_n[at, :] = outside(side, rows[2 * STEPS : 3 * STEPS]) * 0.5

    sublane = lax.broadcasted_iota(jnp.int32, (8, 128), 0)
    lane = lax.broadcasted_iota(jnp.int32, (8, 128), 1)
    tiles = NLON // 128

    def strips(ref, r):
        whole = ref[pl.ds(r, 8), :]
        return [whole[:, 128 * v : 128 * (v + 1)] for v in range(tiles)]

    def row_above(before, x):
        return pltpu.roll(jnp.where(sublane == 7, before, x), 1, 0)

    def row_below(x, behind):
        return pltpu.roll(jnp.where(sublane == 0, behind, x), 7, 0)

    def forward_strip(src, dst, r):
        before, x, behind = strips(src, r - 8), strips(src, r), strips(src, r + 8)
        he, hn = strips(half_e, r), strips(half_n, r)
        right = [None] * tiles
        left = [None] * tiles
        out = []
        for v in range(tiles):
            for w in (v - 1, v, v + 1):
                w = w % tiles
                if right[w] is None:
                    right[w], left[w] = pltpu.roll(x[w], 1, 1), pltpu.roll(x[w], 127, 1)
            above = row_above(before[v], x[v])
            below = row_below(x[v], behind[v])
            east = jnp.where(lane == 127, left[(v + 1) % tiles], left[v])
            west = jnp.where(lane == 0, right[v - 1], right[v])
            out.append(
                DIFFUSION * ((x[v] + (east + west)) + (above + below))
                + he[v] * (west - east)
                + hn[v] * (above - below)
            )
        dst[pl.ds(r, 8), :] = jnp.concatenate(out, axis=1)

    def adjoint_strip(src, dst, r):
        before, y, behind = strips(src, r - 8), strips(src, r), strips(src, r + 8)
        n_before, hn, n_behind = strips(half_n, r - 8), strips(half_n, r), strips(half_n, r + 8)
        he = strips(half_e, r)
        fifth = [None] * tiles
        right = [None] * tiles
        left = [None] * tiles
        out = []
        for v in range(tiles):
            for w in (v - 1, v, v + 1):
                w = w % tiles
                if right[w] is None:
                    fifth[w] = DIFFUSION * y[w]
                    zonal = he[w] * y[w]
                    right[w] = pltpu.roll(fifth[w] - zonal, 1, 1)
                    left[w] = pltpu.roll(fifth[w] + zonal, 127, 1)
            merid = hn[v] * y[v]
            north = row_above((DIFFUSION - n_before[v]) * before[v], fifth[v] - merid)
            south = row_below(fifth[v] + merid, (DIFFUSION + n_behind[v]) * behind[v])
            east = jnp.where(lane == 127, left[(v + 1) % tiles], left[v])
            west = jnp.where(lane == 0, right[v - 1], right[v])
            out.append(fifth[v] + (north + south) + (east + west))
        dst[pl.ds(r, 8), :] = jnp.concatenate(out, axis=1)

    def steps(strip):
        for step in range(STEPS):
            src, dst = (state, state_b) if step % 2 == 0 else (state_b, state)
            whole = step < STEPS - 1

            def one(i, _):
                r = pl.multiple_of(8 * i + (TOP - 8 if whole else TOP), 8)
                strip(src, dst, r)
                return 0

            count = ROWS // 8 + (2 if whole else 0)
            lax.fori_loop(0, count, one, 0, unroll=count // 2)
            if whole:
                for side in range(2):
                    at = pl.ds(halo_at[side], 8)
                    dst[at, :] = jnp.where(inside[side], dst[at, :], 0.0)

    for at in (TOP - 16, TOP + ROWS + 8):
        for ref in (state, state_b, half_n):
            ref[pl.ds(at, 8), :] = jnp.zeros((8, NLON), F32)
    steps(adjoint_strip)
    adj_s[...] = state[TOP : TOP + ROWS, :].astype(BF16)

    @pl.when(has_previous)
    def _():
        adj_copies[0].start()


    loads["var"].wait()
    varf[:, 0:OWN] = var_v[...].astype(F32).T
    varf[:, OWN:CHUNK] = jnp.zeros((NLAT, CHUNK - OWN), F32)
    lat_load.wait()
    latt_load.wait()

    def gather(o, _):
        source = lax.rem(me + o, SPACE)

        @pl.when(o > 0)
        def _():
            pltpu.make_async_remote_copy(
                src_ref=send1.at[0], dst_ref=recv1.at[source],
                send_sem=a1_ss.at[0], recv_sem=a1_rs.at[source],
                device_id=(tm, source), device_id_type=MESH,
            ).wait_recv()

        at = pl.multiple_of(source * ROWS, 16)
        cols[pl.ds(at, ROWS), 0:MAIN] = recv1[source, 0:ROWS, :]
        tail = recv1[source, ROWS:MSG, :].astype(F32)
        for g in range(5):
            rows = turned(tail[0:16], -TAIL * g) if g < 4 else tail[16:32]
            cols[pl.ds(pl.multiple_of(at + 16 * g, 16), 16), MAIN:CHUNK] = rows.astype(BF16)
        return 0

    lax.fori_loop(0, SPACE, gather, 0)

    def lat_step(m, _):
        at = pl.ds(pl.multiple_of(m * 320, 320), 320)
        product = jnp.dot(lat_v[m], cols[...], preferred_element_type=F32)
        scaled[at, :] = (product * varf[at, :]).astype(BF16)
        return 0

    lax.fori_loop(0, 4, lat_step, 0)

    def a2_copy(slot, owner):
        return pltpu.make_async_remote_copy(
            src_ref=send2.at[slot], dst_ref=recv2.at[me],
            send_sem=a2_ss.at[slot], recv_sem=a2_rs.at[me],
            device_id=(tm, owner), device_id_type=MESH,
        )

    def back_step(j, _):
        q = lax.rem(band + 1 + j, 4)
        product = jnp.dot(latt_v[q], scaled[...], preferred_element_type=F32)
        for r in range(4):
            block = product[ROWS * r : ROWS * (r + 1)]
            tile = block[:, MAIN:CHUNK]
            send2[4 * j + r, 0:ROWS, :] = block[:, 0:MAIN].astype(BF16)
            send2[4 * j + r, ROWS:MSG, :] = packed_tail(
                [tile[16 * g : 16 * (g + 1)] for g in range(5)], 0
            )

        @pl.when(j < 3)
        def _():
            for r in range(4):
                a2_copy(4 * j + r, 4 * q + r).start()

        return 0

    lax.fori_loop(0, 4, back_step, 0)
    for o in range(1, 4):
        other = lax.rem(seat + o, 4)
        a2_copy(12 + other, 4 * band + other).start()
    recv2[me] = send2[12 + seat]

    @pl.when(has_previous)
    def _():
        adj_copies[1].start()


    @pl.when(has_previous)
    def _():
        for copy in (*inc_copies, edge_copies[1], edge_copies[3]):
            copy.wait_recv()

    @pl.when(jnp.logical_not(has_previous))
    def _():
        inc_r[...] = jnp.zeros_like(inc_r)
        inc_edge_r[...] = jnp.zeros_like(inc_edge_r)

    state[TOP : TOP + ROWS, :] = inc_r[...].astype(F32)
    for side in range(2):
        rows = inc_edge_r[side].astype(F32)
        rows = jnp.concatenate([rows[STEPS * q : STEPS * (q + 1)] for q in range(4)], axis=1)
        state[pl.ds(halo_at[side], 8), :] = jnp.where(inside[side], outside(side, rows), 0.0)
    steps(forward_strip)

    for source in range(SPACE):

        @pl.when(source != me)
        def _():
            pltpu.make_async_remote_copy(
                src_ref=send2.at[0], dst_ref=recv2.at[source],
                send_sem=a2_ss.at[0], recv_sem=a2_rs.at[source],
                device_id=(tm, me), device_id_type=MESH,
            ).wait_recv()

    place = lane_group((16, 128))
    for q in range(4):
        tails = []
        for r in range(4):
            source = 4 * q + r
            grid[:, MAIN * source : MAIN * (source + 1)] = recv2[source, 0:ROWS, :]
            tails.append(recv2[source, ROWS:MSG, :].astype(F32))
        for g in range(5):
            rows = jnp.zeros((16, 128), F32)
            for r in range(4):
                part = tails[r][0:16] if g < 4 else tails[r][16:32]
                rows = jnp.where(place == r, turned(part, TAIL * (r - g % 4)), rows)
            at = SPACE * MAIN + 128 * q
            grid[16 * g : 16 * (g + 1), at : at + 128] = rows.astype(BF16)

    def out_step(n, _):
        pltpu.make_async_copy(loni_h.at[n], loni_v.at[n], loni_sem.at[n]).wait()
        at = pl.ds(pl.multiple_of(n * CHUNK, CHUNK), CHUNK)
        term = jnp.dot(grid[...], loni_v[n], preferred_element_type=F32)
        ahead = state[TOP : TOP + ROWS, at]
        out1_v[:, at] = term + inc_v[:, at].astype(F32) - ahead
        pltpu.make_async_copy(out1_v.at[:, at], out1_h.at[:, at], out1_sem.at[n]).start()
        return 0

    lax.fori_loop(0, CHUNKS, out_step, 0)
    @pl.when(has_next)
    def _():
        for copy in adj_copies:
            copy.wait_recv()

    @pl.when(jnp.logical_not(has_next))
    def _():
        adj_r[...] = jnp.zeros_like(adj_r)

    out2_copy = load(adj_r, out2_h, load_sem.at[7])

    for copy in (edge_copies[0], edge_copies[2]):
        copy.wait_send()

    @pl.when(has_next)
    def _():
        for copy in (*inc_copies, edge_copies[1], edge_copies[3]):
            copy.wait_send()

    @pl.when(has_previous)
    def _():
        for copy in adj_copies:
            copy.wait_send()


    def sent(slot, _):
        for src, dst, ss, rs in ((send1, recv1, a1_ss, a1_rs), (send2, recv2, a2_ss, a2_rs)):
            own = (14 + core) if ss is a1_ss else (12 + seat)

            @pl.when(slot != own)
            def _():
                pltpu.make_async_remote_copy(
                    src_ref=src.at[slot], dst_ref=dst.at[me],
                    send_sem=ss.at[slot], recv_sem=rs.at[me],
                    device_id=(tm, sibling), device_id_type=MESH,
                ).wait_send()

        return 0

    lax.fori_loop(0, SPACE, sent, 0)
    out2_copy.wait()

    def written(n, _):
        at = pl.ds(pl.multiple_of(n * CHUNK, CHUNK), CHUNK)
        pltpu.make_async_copy(out1_v.at[:, at], out1_h.at[:, at], out1_sem.at[n]).wait()
        return 0

    lax.fori_loop(0, CHUNKS, written, 0)


def shards(windows, multiplier, increment, wind_east, wind_north, variances):
    lonf, loni, lat, latt = (jnp.asarray(table) for table in tables())
    block = (ROWS, NLON)
    wide = (PADDED, NLON)
    dma = pltpu.SemaphoreType.DMA
    vmem = pltpu.VMEM
    first, last = pl.pallas_call(
        functools.partial(kernel, windows),
        out_shape=(jax.ShapeDtypeStruct(block, F32), jax.ShapeDtypeStruct(block, BF16)),
        in_specs=[pl.BlockSpec(memory_space=pl.ANY)] * 9,
        out_specs=(pl.BlockSpec(memory_space=pl.ANY),) * 2,
        scratch_shapes=[
            vmem(block, BF16), vmem(block, BF16), vmem(block, BF16), vmem(block, BF16),
            vmem((OWN, NLAT), BF16),
            vmem((CHUNKS, NLON, CHUNK), BF16), vmem((CHUNKS, NLON, CHUNK), BF16),
            vmem((4, 320, NLAT), BF16), vmem((4, 320, NLAT), BF16),
            vmem(block, BF16), vmem((2, 16, 640), BF16), vmem((2, 16, 640), BF16),
            vmem((2, 16, NLON), BF16), vmem((2, 16, NLON), BF16),
            vmem(block, BF16), vmem(block, BF16),
            vmem(wide, F32), vmem(wide, F32), vmem(wide, F32), vmem(wide, F32),
            vmem((SPACE, MSG, 128), BF16), vmem((SPACE, MSG, 128), BF16),
            vmem((SPACE, MSG, 128), BF16), vmem((SPACE, MSG, 128), BF16),
            vmem((NLAT, CHUNK), BF16), vmem((NLAT, CHUNK), BF16), vmem(block, BF16),
            vmem((NLAT, CHUNK), F32), vmem(block, F32),
            dma((8,)), dma((CHUNKS,)), dma((CHUNKS,)), dma((CHUNKS,)),
            dma((4,)), dma((2,)), dma((2,)), dma((2,)), dma((2,)), dma((4,)),
            dma((SPACE,)), dma((SPACE,)), dma((SPACE,)), dma((SPACE,)),
        ],
        compiler_params=pltpu.CompilerParams(
            collective_id=0, has_side_effects=True, vmem_limit_bytes=60 * 2**20
        ),
        cost_estimate=pl.CostEstimate(
            flops=3_145_728_000, bytes_accessed=36_000_000, transcendentals=0
        ),
    )(
        multiplier[0], increment[0], wind_east[0], wind_north[0],
        jnp.swapaxes(variances[0], 0, 1), lonf, loni, lat, latt,
    )
    last = (multiplier[0].astype(F32) - last.astype(F32)).astype(BF16)
    return first.astype(BF16)[None], last[None]


def solution(mesh):
    placed = P("tm", "space", None)
    return jax.shard_map(
        functools.partial(shards, mesh.shape["tm"]),
        mesh=mesh,
        in_specs=(placed, placed, placed, placed, P("tm", None, "space")),
        out_specs=(placed, placed),
        check_vma=False,
    )
```

```python
import functools
import math

import jax
import jax.numpy as jnp
import ml_dtypes
import numpy as np
from jax import lax
from jax.experimental import pallas as pl
from jax.experimental.pallas import tpu as pltpu
from jax.sharding import PartitionSpec as P

STEPS = 4
DIFFUSION = 0.2
MESH = pl.DeviceIdType.MESH

ROWS = 80
NLON = 2560
NLAT = 1280
SPACE = 16
OWN = NLON // SPACE
MAIN = 128
TAIL = OWN - MAIN
MSG = 112
TOP = 16
PADDED = ROWS + 32
CHUNK = 256
CHUNKS = NLON // CHUNK
INC_CUT = 16
ADJ_CUT = 64
F32 = jnp.float32
BF16 = jnp.bfloat16


def longitude_table():
    row = np.arange(NLON)[:, None]
    col = np.arange(NLON)[None, :]
    half = NLON // 2
    wave = np.where(col <= half, col, col - half)
    angle = (wave * row % NLON) * (2.0 * math.pi / NLON)
    scale = np.where((col == 0) | (col == half), math.sqrt(1.0 / NLON), math.sqrt(2.0 / NLON))
    return (np.where(col <= half, np.cos(angle), np.sin(angle)) * scale).astype(ml_dtypes.bfloat16)


def latitude_table():
    mode = np.arange(NLAT)[:, None]
    row = np.arange(NLAT)[None, :]
    angle = (mode * (2 * row + 1) % (4 * NLAT)) * (math.pi / (2.0 * NLAT))
    scale = np.where(mode == 0, math.sqrt(1.0 / NLAT), math.sqrt(2.0 / NLAT))
    return (np.cos(angle) * scale).astype(ml_dtypes.bfloat16)


def column_order():
    first = [OWN * d + np.arange(MAIN) for d in range(SPACE)]
    last = [OWN * d + MAIN + np.arange(TAIL) for d in range(SPACE)]
    return np.concatenate(first + last)


@functools.lru_cache(maxsize=1)
def tables():
    lon = longitude_table()
    lat = latitude_table()
    order = column_order()
    forward = lon[:, order].reshape(NLON, CHUNKS, CHUNK).transpose(1, 0, 2)
    inverse = lon.T[order, :].reshape(NLON, CHUNKS, CHUNK).transpose(1, 0, 2)
    return (
        np.ascontiguousarray(forward),
        np.ascontiguousarray(inverse),
        np.ascontiguousarray(lat.reshape(4, 320, NLAT)),
        np.ascontiguousarray(lat.T.reshape(4, 320, NLAT)),
    )


def lane_group(shape):
    return lax.broadcasted_iota(jnp.int32, shape, 1) // TAIL


def turned(x, shift):
    shift = shift % x.shape[1]
    return x if shift == 0 else pltpu.roll(x, shift, 1)


def packed_tail(groups, from_group):
    place = lane_group((16, 128))
    head = jnp.zeros((16, 128), F32)
    for g in range(4):
        head = jnp.where(place == g, turned(groups[g], TAIL * (g - from_group)), head)
    last = turned(groups[4], TAIL * (0 - from_group))
    return jnp.concatenate([head, last], axis=0).astype(BF16)


def kernel(
    windows,
    mult_h, inc_h, east_h, north_h, var_h, lonf_h, loni_h, lat_h, latt_h,
    out1_h, out2_h,
    mult_v, inc_v, east_v, north_v, var_v, lonf_v, loni_v, lat_v, latt_v,
    inc_r, inc_edge_s, inc_edge_r, edge_s, edge_r, adj_s, adj_r,
    state, state_b, half_e, half_n,
    send1, recv1, send2, recv2,
    cols, scaled, grid, varf, out1_v,
    load_sem, lonf_sem, loni_sem, out1_sem,
    inc_sem, iedge_ss, iedge_rs, edge_ss, edge_rs, adj_sem,
    a1_ss, a1_rs, a2_ss, a2_rs,
):
    tm = lax.axis_index("tm")
    me = lax.axis_index("space")
    after = lax.rem(tm + 1, windows)
    before = lax.rem(tm + windows - 1, windows)
    up = lax.rem(me + SPACE - 1, SPACE)
    down = lax.rem(me + 1, SPACE)
    core = lax.rem(me, 2)
    chip = me // 2
    sibling = me + 1 - 2 * core
    band = me // 4
    seat = lax.rem(me, 4)

    barrier = pltpu.get_barrier_semaphore()
    for o in range(1, SPACE):
        pl.semaphore_signal(
            barrier, inc=1, device_id=(tm, lax.rem(me + o, SPACE)), device_id_type=MESH
        )
    for window in (after, before):
        for space in (me, up, down):
            pl.semaphore_signal(barrier, inc=1, device_id=(window, space), device_id_type=MESH)

    def load(src, dst, sem):
        copy = pltpu.make_async_copy(src, dst, sem)
        copy.start()
        return copy

    loads = {
        name: load(src, dst, load_sem.at[n])
        for n, (name, src, dst) in enumerate(
            (
                ("mult", mult_h, mult_v),
                ("inc", inc_h, inc_v),
                ("east", east_h, east_v),
                ("north", north_h, north_v),
            )
        )
    }
    lonf_loads = [load(lonf_h.at[8 + t], lonf_v.at[8 + t], lonf_sem.at[8 + t]) for t in range(2)]
    for j in range(8):
        which = lax.rem(chip + 1 + j, 8)
        lonf_loads.append(load(lonf_h.at[which], lonf_v.at[j], lonf_sem.at[j]))

    loads["var"] = load(var_h, var_v, load_sem.at[4])
    lat_load = load(lat_h, lat_v, load_sem.at[5])
    latt_load = load(latt_h, latt_v, load_sem.at[6])
    for n in range(CHUNKS):
        load(loni_h.at[n], loni_v.at[n], loni_sem.at[n])

    pl.semaphore_wait(barrier, 21)

    def exchange(src, dst, sem, to, cut):
        return [
            pltpu.make_async_remote_copy(
                src_ref=src.at[rows], dst_ref=dst.at[rows],
                send_sem=sem.at[2 * n], recv_sem=sem.at[2 * n + 1],
                device_id=(to, me), device_id_type=MESH,
            )
            for n, rows in enumerate((pl.ds(0, cut), pl.ds(cut, ROWS - cut)))
        ]

    inc_copies = exchange(inc_v, inc_r, inc_sem, after, INC_CUT)
    adj_copies = exchange(adj_s, adj_r, adj_sem, before, ADJ_CUT)
    has_next, has_previous = tm < windows - 1, tm > 0

    def edges(ref):
        first = ref[0:16, :].astype(F32)[0:STEPS]
        last = ref[ROWS - 16 : ROWS, :].astype(F32)[16 - STEPS : 16]
        return first, last

    def folded(rows):
        return jnp.concatenate([rows[:, 640 * q : 640 * (q + 1)] for q in range(4)], axis=0)

    for name in ("mult", "inc", "east", "north"):
        loads[name].wait()
    parts = [edges(ref) for ref in (mult_v, east_v, north_v)]
    blank = jnp.zeros((16 - 3 * STEPS, NLON), F32)
    for side in range(2):
        edge_s[side] = jnp.concatenate([part[side] for part in parts] + [blank], axis=0).astype(BF16)
    own_edges = edges(inc_v)
    for side in range(2):
        inc_edge_s[side] = folded(own_edges[side]).astype(BF16)
    edge_copies = []
    for side, space in ((0, up), (1, down)):
        edge_copies.append(
            pltpu.make_async_remote_copy(
                src_ref=edge_s.at[side], dst_ref=edge_r.at[1 - side],
                send_sem=edge_ss.at[side], recv_sem=edge_rs.at[1 - side],
                device_id=(tm, space), device_id_type=MESH,
            )
        )
        edge_copies.append(
            pltpu.make_async_remote_copy(
                src_ref=inc_edge_s.at[side], dst_ref=inc_edge_r.at[1 - side],
                send_sem=iedge_ss.at[side], recv_sem=iedge_rs.at[1 - side],
                device_id=(after, space), device_id_type=MESH,
            )
        )
    for copy in (edge_copies[0], edge_copies[2]):
        copy.start()

    @pl.when(has_next)
    def _():
        for copy in (edge_copies[1], edge_copies[3]):
            copy.start()


    for t in range(2):
        lonf_loads[t].wait()
        product = jnp.dot(mult_v[...], lonf_v[8 + t], preferred_element_type=F32)
        for q in range(2):
            tile = product[:, 128 * q : 128 * (q + 1)]
            groups = [tile[16 * g : 16 * (g + 1)] for g in range(5)]
            for r in range(4):
                recv_slot = 4 * (2 * t + q) + r
                slot = 2 * lax.rem(recv_slot // 2 + 15 - chip, 8) + recv_slot % 2
                send1[slot, ROWS:MSG, :] = packed_tail(groups, r)

    def a1_copy(slot, owner):
        return pltpu.make_async_remote_copy(
            src_ref=send1.at[slot], dst_ref=recv1.at[me],
            send_sem=a1_ss.at[slot], recv_sem=a1_rs.at[me],
            device_id=(tm, owner), device_id_type=MESH,
        )

    def lon_step(j, _):
        which = lax.rem(chip + 1 + j, 8)
        pltpu.make_async_copy(lonf_h.at[which], lonf_v.at[j], lonf_sem.at[j]).wait()
        product = jnp.dot(mult_v[...], lonf_v[j], preferred_element_type=F32).astype(BF16)
        for c in range(2):
            send1[2 * j + c, 0:ROWS, :] = product[:, 128 * c : 128 * (c + 1)]

        @pl.when(j < 7)
        def _():
            for c in range(2):
                a1_copy(2 * j + c, 2 * which + c).start()

        return 0

    lax.fori_loop(0, 8, lon_step, 0)
    a1_copy(14 + 1 - core, sibling).start()
    recv1[me] = send1[14 + core]

    @pl.when(has_next)
    def _():
        for copy in inc_copies:
            copy.start()


    for ref, src in ((half_e, east_v), (half_n, north_v)):
        ref[TOP : TOP + ROWS, :] = src[...].astype(F32) * 0.5
    state[TOP : TOP + ROWS, :] = mult_v[...].astype(F32)
    for side in range(2):
        edge_copies[2 * side].wait_recv()
    gap = jnp.zeros((8 - STEPS, NLON), F32)

    def outside(side, rows):
        parts = [gap, rows] if side == 0 else [rows, gap]
        return jnp.concatenate(parts, axis=0)

    halo_at = (TOP - 8, TOP + ROWS)
    inside = (me > 0, me < SPACE - 1)
    for side in range(2):
        rows = edge_r[side].astype(F32)
        at = pl.ds(halo_at[side], 8)
        state[at, :] = jnp.where(inside[side], outside(side, rows[0:STEPS]), 0.0)
        half_e[at, :] = outside(side, rows[STEPS : 2 * STEPS]) * 0.5
        half_n[at, :] = outside(side, rows[2 * STEPS : 3 * STEPS]) * 0.5

    sublane = lax.broadcasted_iota(jnp.int32, (8, 128), 0)
    lane = lax.broadcasted_iota(jnp.int32, (8, 128), 1)
    tiles = NLON // 128

    def strips(ref, r):
        whole = ref[pl.ds(r, 8), :]
        return [whole[:, 128 * v : 128 * (v + 1)] for v in range(tiles)]

    def row_above(before, x):
        return pltpu.roll(jnp.where(sublane == 7, before, x), 1, 0)

    def row_below(x, behind):
        return pltpu.roll(jnp.where(sublane == 0, behind, x), 7, 0)

    def forward_strip(src, dst, r):
        before, x, behind = strips(src, r - 8), strips(src, r), strips(src, r + 8)
        he, hn = strips(half_e, r), strips(half_n, r)
        right = [None] * tiles
        left = [None] * tiles
        out = []
        for v in range(tiles):
            for w in (v - 1, v, v + 1):
                w = w % tiles
                if right[w] is None:
                    right[w], left[w] = pltpu.roll(x[w], 1, 1), pltpu.roll(x[w], 127, 1)
            above = row_above(before[v], x[v])
            below = row_below(x[v], behind[v])
            east = jnp.where(lane == 127, left[(v + 1) % tiles], left[v])
            west = jnp.where(lane == 0, right[v - 1], right[v])
            out.append(
                DIFFUSION * ((x[v] + (east + west)) + (above + below))
                + he[v] * (west - east)
                + hn[v] * (above - below)
            )
        dst[pl.ds(r, 8), :] = jnp.concatenate(out, axis=1)

    def adjoint_strip(src, dst, r):
        before, y, behind = strips(src, r - 8), strips(src, r), strips(src, r + 8)
        n_before, hn, n_behind = strips(half_n, r - 8), strips(half_n, r), strips(half_n, r + 8)
        he = strips(half_e, r)
        fifth = [None] * tiles
        right = [None] * tiles
        left = [None] * tiles
        out = []
        for v in range(tiles):
            for w in (v - 1, v, v + 1):
                w = w % tiles
                if right[w] is None:
                    fifth[w] = DIFFUSION * y[w]
                    zonal = he[w] * y[w]
                    right[w] = pltpu.roll(fifth[w] - zonal, 1, 1)
                    left[w] = pltpu.roll(fifth[w] + zonal, 127, 1)
            merid = hn[v] * y[v]
            north = row_above((DIFFUSION - n_before[v]) * before[v], fifth[v] - merid)
            south = row_below(fifth[v] + merid, (DIFFUSION + n_behind[v]) * behind[v])
            east = jnp.where(lane == 127, left[(v + 1) % tiles], left[v])
            west = jnp.where(lane == 0, right[v - 1], right[v])
            out.append(fifth[v] + (north + south) + (east + west))
        dst[pl.ds(r, 8), :] = jnp.concatenate(out, axis=1)

    def steps(strip):
        for step in range(STEPS):
            src, dst = (state, state_b) if step % 2 == 0 else (state_b, state)
            whole = step < STEPS - 1

            def one(i, _):
                r = pl.multiple_of(8 * i + (TOP - 8 if whole else TOP), 8)
                strip(src, dst, r)
                return 0

            count = ROWS // 8 + (2 if whole else 0)
            lax.fori_loop(0, count, one, 0, unroll=count // 2)
            if whole:
                for side in range(2):
                    at = pl.ds(halo_at[side], 8)
                    dst[at, :] = jnp.where(inside[side], dst[at, :], 0.0)

    for at in (TOP - 16, TOP + ROWS + 8):
        for ref in (state, state_b, half_n):
            ref[pl.ds(at, 8), :] = jnp.zeros((8, NLON), F32)
    steps(adjoint_strip)
    adj_s[...] = state[TOP : TOP + ROWS, :].astype(BF16)

    @pl.when(has_previous)
    def _():
        adj_copies[0].start()


    loads["var"].wait()
    varf[:, 0:OWN] = var_v[...].astype(F32).T
    varf[:, OWN:CHUNK] = jnp.zeros((NLAT, CHUNK - OWN), F32)
    lat_load.wait()
    latt_load.wait()

    def gather(o, _):
        source = lax.rem(me + o, SPACE)

        @pl.when(o > 0)
        def _():
            pltpu.make_async_remote_copy(
                src_ref=send1.at[0], dst_ref=recv1.at[source],
                send_sem=a1_ss.at[0], recv_sem=a1_rs.at[source],
                device_id=(tm, source), device_id_type=MESH,
            ).wait_recv()

        at = pl.multiple_of(source * ROWS, 16)
        cols[pl.ds(at, ROWS), 0:MAIN] = recv1[source, 0:ROWS, :]
        tail = recv1[source, ROWS:MSG, :].astype(F32)
        for g in range(5):
            rows = turned(tail[0:16], -TAIL * g) if g < 4 else tail[16:32]
            cols[pl.ds(pl.multiple_of(at + 16 * g, 16), 16), MAIN:CHUNK] = rows.astype(BF16)
        return 0

    lax.fori_loop(0, SPACE, gather, 0)

    def lat_step(m, _):
        at = pl.ds(pl.multiple_of(m * 320, 320), 320)
        product = jnp.dot(lat_v[m], cols[...], preferred_element_type=F32)
        scaled[at, :] = (product * varf[at, :]).astype(BF16)
        return 0

    lax.fori_loop(0, 4, lat_step, 0)

    def a2_copy(slot, owner):
        return pltpu.make_async_remote_copy(
            src_ref=send2.at[slot], dst_ref=recv2.at[me],
            send_sem=a2_ss.at[slot], recv_sem=a2_rs.at[me],
            device_id=(tm, owner), device_id_type=MESH,
        )

    def back_step(j, _):
        q = lax.rem(band + 1 + j, 4)
        product = jnp.dot(latt_v[q], scaled[...], preferred_element_type=F32)
        for r in range(4):
            block = product[ROWS * r : ROWS * (r + 1)]
            tile = block[:, MAIN:CHUNK]
            send2[4 * j + r, 0:ROWS, :] = block[:, 0:MAIN].astype(BF16)
            send2[4 * j + r, ROWS:MSG, :] = packed_tail(
                [tile[16 * g : 16 * (g + 1)] for g in range(5)], 0
            )

        @pl.when(j < 3)
        def _():
            for r in range(4):
                a2_copy(4 * j + r, 4 * q + r).start()

        return 0

    lax.fori_loop(0, 4, back_step, 0)
    for o in range(1, 4):
        other = lax.rem(seat + o, 4)
        a2_copy(12 + other, 4 * band + other).start()
    recv2[me] = send2[12 + seat]

    @pl.when(has_previous)
    def _():
        adj_copies[1].start()


    @pl.when(has_previous)
    def _():
        for copy in (*inc_copies, edge_copies[1], edge_copies[3]):
            copy.wait_recv()

    @pl.when(jnp.logical_not(has_previous))
    def _():
        inc_r[...] = jnp.zeros_like(inc_r)
        inc_edge_r[...] = jnp.zeros_like(inc_edge_r)

    state[TOP : TOP + ROWS, :] = inc_r[...].astype(F32)
    for side in range(2):
        rows = inc_edge_r[side].astype(F32)
        rows = jnp.concatenate([rows[STEPS * q : STEPS * (q + 1)] for q in range(4)], axis=1)
        state[pl.ds(halo_at[side], 8), :] = jnp.where(inside[side], outside(side, rows), 0.0)
    steps(forward_strip)

    for source in range(SPACE):

        @pl.when(source != me)
        def _():
            pltpu.make_async_remote_copy(
                src_ref=send2.at[0], dst_ref=recv2.at[source],
                send_sem=a2_ss.at[0], recv_sem=a2_rs.at[source],
                device_id=(tm, me), device_id_type=MESH,
            ).wait_recv()

    place = lane_group((16, 128))
    for q in range(4):
        tails = []
        for r in range(4):
            source = 4 * q + r
            grid[:, MAIN * source : MAIN * (source + 1)] = recv2[source, 0:ROWS, :]
            tails.append(recv2[source, ROWS:MSG, :].astype(F32))
        for g in range(5):
            rows = jnp.zeros((16, 128), F32)
            for r in range(4):
                part = tails[r][0:16] if g < 4 else tails[r][16:32]
                rows = jnp.where(place == r, turned(part, TAIL * (r - g % 4)), rows)
            at = SPACE * MAIN + 128 * q
            grid[16 * g : 16 * (g + 1), at : at + 128] = rows.astype(BF16)

    def out_step(n, _):
        pltpu.make_async_copy(loni_h.at[n], loni_v.at[n], loni_sem.at[n]).wait()
        at = pl.ds(pl.multiple_of(n * CHUNK, CHUNK), CHUNK)
        term = jnp.dot(grid[...], loni_v[n], preferred_element_type=F32)
        ahead = state[TOP : TOP + ROWS, at]
        out1_v[:, at] = term + inc_v[:, at].astype(F32) - ahead
        pltpu.make_async_copy(out1_v.at[:, at], out1_h.at[:, at], out1_sem.at[n]).start()
        return 0

    lax.fori_loop(0, CHUNKS, out_step, 0)
    @pl.when(has_next)
    def _():
        for copy in adj_copies:
            copy.wait_recv()

    @pl.when(jnp.logical_not(has_next))
    def _():
        adj_r[...] = jnp.zeros_like(adj_r)

    out2_copy = load(adj_r, out2_h, load_sem.at[7])

    for copy in (edge_copies[0], edge_copies[2]):
        copy.wait_send()

    @pl.when(has_next)
    def _():
        for copy in (*inc_copies, edge_copies[1], edge_copies[3]):
            copy.wait_send()

    @pl.when(has_previous)
    def _():
        for copy in adj_copies:
            copy.wait_send()


    def sent(slot, _):
        for src, dst, ss, rs in ((send1, recv1, a1_ss, a1_rs), (send2, recv2, a2_ss, a2_rs)):
            own = (14 + core) if ss is a1_ss else (12 + seat)

            @pl.when(slot != own)
            def _():
                pltpu.make_async_remote_copy(
                    src_ref=src.at[slot], dst_ref=dst.at[me],
                    send_sem=ss.at[slot], recv_sem=rs.at[me],
                    device_id=(tm, sibling), device_id_type=MESH,
                ).wait_send()

        return 0

    lax.fori_loop(0, SPACE, sent, 0)
    out2_copy.wait()

    def written(n, _):
        at = pl.ds(pl.multiple_of(n * CHUNK, CHUNK), CHUNK)
        pltpu.make_async_copy(out1_v.at[:, at], out1_h.at[:, at], out1_sem.at[n]).wait()
        return 0

    lax.fori_loop(0, CHUNKS, written, 0)


def shards(windows, multiplier, increment, wind_east, wind_north, variances):
    lonf, loni, lat, latt = (jnp.asarray(table) for table in tables())
    block = (ROWS, NLON)
    wide = (PADDED, NLON)
    dma = pltpu.SemaphoreType.DMA
    vmem = pltpu.VMEM
    first, last = pl.pallas_call(
        functools.partial(kernel, windows),
        out_shape=(jax.ShapeDtypeStruct(block, F32), jax.ShapeDtypeStruct(block, BF16)),
        in_specs=[pl.BlockSpec(memory_space=pl.ANY)] * 9,
        out_specs=(pl.BlockSpec(memory_space=pl.ANY),) * 2,
        scratch_shapes=[
            vmem(block, BF16), vmem(block, BF16), vmem(block, BF16), vmem(block, BF16),
            vmem((OWN, NLAT), BF16),
            vmem((CHUNKS, NLON, CHUNK), BF16), vmem((CHUNKS, NLON, CHUNK), BF16),
            vmem((4, 320, NLAT), BF16), vmem((4, 320, NLAT), BF16),
            vmem(block, BF16), vmem((2, 16, 640), BF16), vmem((2, 16, 640), BF16),
            vmem((2, 16, NLON), BF16), vmem((2, 16, NLON), BF16),
            vmem(block, BF16), vmem(block, BF16),
            vmem(wide, F32), vmem(wide, F32), vmem(wide, F32), vmem(wide, F32),
            vmem((SPACE, MSG, 128), BF16), vmem((SPACE, MSG, 128), BF16),
            vmem((SPACE, MSG, 128), BF16), vmem((SPACE, MSG, 128), BF16),
            vmem((NLAT, CHUNK), BF16), vmem((NLAT, CHUNK), BF16), vmem(block, BF16),
            vmem((NLAT, CHUNK), F32), vmem(block, F32),
            dma((8,)), dma((CHUNKS,)), dma((CHUNKS,)), dma((CHUNKS,)),
            dma((4,)), dma((2,)), dma((2,)), dma((2,)), dma((2,)), dma((4,)),
            dma((SPACE,)), dma((SPACE,)), dma((SPACE,)), dma((SPACE,)),
        ],
        compiler_params=pltpu.CompilerParams(
            collective_id=0, has_side_effects=True, vmem_limit_bytes=60 * 2**20
        ),
        cost_estimate=pl.CostEstimate(
            flops=3_145_728_000, bytes_accessed=36_000_000, transcendentals=0
        ),
    )(
        multiplier[0], increment[0], wind_east[0], wind_north[0],
        jnp.swapaxes(variances[0], 0, 1), lonf, loni, lat, latt,
    )
    last = (multiplier[0].astype(F32) - last.astype(F32)).astype(BF16)
    return first.astype(BF16)[None], last[None]


def solution(mesh):
    placed = P("tm", "space", None)
    return jax.shard_map(
        functools.partial(shards, mesh.shape["tm"]),
        mesh=mesh,
        in_specs=(placed, placed, placed, placed, P("tm", None, "space")),
        out_specs=(placed, placed),
        check_vma=False,
    )
```
